32 devices in a mesh: tok: 16 (over z, x, core), mlp: 2 (over y).
Axes of the slice: x: 2, y: 2, z: 4, core: 2. Of those that a mesh axis runs over, the one named last changes fastest.
Arguments:
- queries: bfloat16 [1024, 7168], P('tok', 'mlp')
- fresh_token_keys: bfloat16 [1024, 1024], P('tok', 'mlp'), may hold values from -6 to 6
- fresh_token_values: bfloat16 [1024, 1024], P('tok', 'mlp'), may hold values from -6 to 6
- leaf_key_block: bfloat16 [5120, 1024], P('tok', 'mlp'), may hold values from -6 to 6
- leaf_value_block: bfloat16 [5120, 1024], P('tok', 'mlp'), may hold values from -6 to 6
- shared_key_block: bfloat16 [4096, 1024], P('tok', 'mlp'), may hold values from -6 to 6
- shared_value_block: bfloat16 [4096, 1024], P('tok', 'mlp'), may hold values from -6 to 6
- out_weight: bfloat16 [7168, 7168], P('mlp', 'tok'), may hold values from -0.0625 to 0.0625
- residual: bfloat16 [1024, 7168], P('mlp', 'tok'), may hold values from -2.5 to 2.5
- token_request: int32 [1024], replicated, may hold values from 0 to 15, as said below
- positions: int32 [1024], P('tok'), may hold values from 129 to 831, as said below
- parents: int32 [26], replicated, may hold values from -1 to 9, as said below
- node_lengths: int32 [26], replicated, may hold values from 1 to 256, as said below
- node_owner: int32 [26], replicated, may hold values from 0 to 15, as said below
Outputs:
- hidden: bfloat16 [1024, 7168], P('mlp', 'tok')
- leaf_key_output: bfloat16 [5120, 1024], P('tok', 'mlp')
- leaf_value_output: bfloat16 [5120, 1024], P('tok', 'mlp')
The draws below stay inside these ranges and needn't reach their ends.
Inputs may be any that keep to these rules, and one draw needn't show every extreme that they name: `token_request`: index d of tok holds the 64 new tokens of the request whose leaf it owns (node_owner of that leaf is d), in some order. positions = node_lengths of the token's root, middle and leaf plus the token's rank among its request's new tokens; the ranks of one request are 0 to 63, each once. `parents`: nodes 0 to 1 are roots (parent -1), the next 8 are middle nodes with a root as parent, the last 16 are the leaves of requests 0, 1, ... with a middle node as parent; every root and middle node has a child; the leaf of request 0 lies below root 0. `node_lengths`: roots and middle nodes hold 64 to 256 tokens, root 0 and the middle node above leaf 0 exactly 256; leaves hold 1 to 256, leaf 0 exactly 256. `node_owner`: the 10 roots and middle nodes have different owners; the leaves' owners are a permutation of the indices of tok; a node's cache starts at row 0 of its owner's block.
All inputs are finite; a program needn't handle non-finite values.
Results may differ from the reference program's by a relative error of at most 0.012.
Values may be sent and summed in bfloat16 or wider, within the bound.
A program may use at most 64 MiB of HBM per device.

```python
import math
import jax
import jax.numpy as jnp
from jax import lax

D = 7168
HQ = 56
KEY_VALUE_HEADS = 8
HEAD_SIZE = 128
QUERY_PER_GROUP = 7
REQUEST_TOKENS = 64
ROOTS = 2
MIDS = 8
NODE_ROW_LIMIT = 256
LEAF_MAX = 256
REQUEST_COUNT = 16
PACKED_TOKENS = 1024
LEAF_BLOCK_ROWS = 320
N_TOK = 16


def structure(key):
    base = jax.random.fold_in(key, 11)
    keys = jax.random.split(base, 10)
    devs = jnp.arange(REQUEST_COUNT, dtype=jnp.int32)
    mid_ids = jnp.arange(MIDS, dtype=jnp.int32)
    root_of_mid = jnp.where(mid_ids < ROOTS, mid_ids, jax.random.randint(keys[1], (MIDS,), 0, ROOTS))
    root_of_mid = root_of_mid[jax.random.permutation(keys[2], MIDS)].astype(jnp.int32)
    mid_of_leaf = jnp.where(devs < MIDS, devs, jax.random.randint(keys[3], (REQUEST_COUNT,), 0, MIDS))
    mid_of_leaf = mid_of_leaf[jax.random.permutation(keys[4], REQUEST_COUNT)].astype(jnp.int32)
    chosen_mid = jnp.argmax((root_of_mid == 0).astype(jnp.int32)).astype(jnp.int32)
    swap_leaf = jnp.argmax((mid_of_leaf == chosen_mid).astype(jnp.int32)).astype(jnp.int32)
    first_mid = mid_of_leaf[0]
    mid_of_leaf = mid_of_leaf.at[swap_leaf].set(first_mid).at[0].set(chosen_mid)
    parents = jnp.concatenate([-jnp.ones((ROOTS,), jnp.int32), root_of_mid.astype(jnp.int32), (ROOTS + mid_of_leaf).astype(jnp.int32)])
    shared_len = jax.random.randint(keys[5], (ROOTS + MIDS,), NODE_ROW_LIMIT // 4, NODE_ROW_LIMIT + 1).at[0].set(NODE_ROW_LIMIT)
    shared_len = shared_len.at[ROOTS + chosen_mid].set(NODE_ROW_LIMIT)
    leaf_len = jax.random.randint(keys[6], (REQUEST_COUNT,), 1, LEAF_MAX + 1).at[0].set(LEAF_MAX)
    lengths = jnp.concatenate([shared_len, leaf_len]).astype(jnp.int32)
    shared_owner = jax.random.permutation(keys[7], REQUEST_COUNT)[:ROOTS + MIDS]
    leaf_owner = jax.random.permutation(keys[8], REQUEST_COUNT).astype(jnp.int32)
    owners = jnp.concatenate([shared_owner, leaf_owner]).astype(jnp.int32)
    prefix = lengths[ROOTS + MIDS + devs] + lengths[ROOTS + mid_of_leaf] + lengths[root_of_mid[mid_of_leaf]]
    held = jnp.argsort(leaf_owner, stable=True).astype(jnp.int32)
    token_request = jnp.repeat(held, REQUEST_TOKENS).astype(jnp.int32)
    shuffle_keys = jax.random.split(keys[9], REQUEST_COUNT)
    ranks = jax.vmap(lambda k: jax.random.permutation(k, REQUEST_TOKENS))(shuffle_keys).astype(jnp.int32)
    positions = prefix[held][:, None] + ranks
    return (token_request, positions.reshape(-1).astype(jnp.int32), parents, lengths, owners)


def draw_token_request(key, part):
    return structure(key)[0]


def draw_positions(key, part):
    return structure(key)[1]


def draw_parents(key, part):
    return structure(key)[2]


def draw_node_lengths(key, part):
    return structure(key)[3]


def draw_node_owner(key, part):
    return structure(key)[4]


def draw_queries(key, part):
    first_key, second_key = jax.random.split(jax.random.fold_in(key, 3))
    entries = jnp.clip(jax.random.normal(first_key, (PACKED_TOKENS, HQ * HEAD_SIZE), jnp.float32), -4.0, 4.0)
    scales = jnp.exp(jax.random.uniform(second_key, (PACKED_TOKENS, 1), jnp.float32, 0.0, 1.1))
    return (entries * scales).astype(jnp.bfloat16)


def block_levels(stream_key, dims, cuts, least, top_value):
    def one(dim, blocks):
        steps = jax.random.uniform(jax.random.fold_in(jax.random.fold_in(stream_key, 6), dim), (blocks,), jnp.float32, least / len(cuts), top_value / len(cuts))
        return jnp.repeat(jnp.exp(steps), dims[dim] // blocks).reshape((-1,) + (1,) * (len(dims) - dim - 1))

    factor_of = one(*cuts[0])
    for cut in cuts[1:]:
        factor_of = factor_of * one(*cut)
    return factor_of


def noise(rng, dims, spread, reach, shards=(), kind=jnp.bfloat16):
    result = spread * jax.random.normal(rng, dims, jnp.float32)
    if shards:
        result = result * block_levels(rng, dims, shards, -0.22, 0.18)
    return jnp.clip(result, -reach, reach).astype(kind)


def setup_inputs(seed: int = 0) -> dict:
    splits = jax.random.split(jax.random.key(seed), 15)
    return {
        "queries": draw_queries(jax.random.fold_in(splits[14], 71), 0),
        "fresh_token_keys": noise(splits[1], (PACKED_TOKENS, KEY_VALUE_HEADS * HEAD_SIZE), 1.0, 6.0, ((0, 16), (1, 2))),
        "fresh_token_values": noise(splits[2], (PACKED_TOKENS, KEY_VALUE_HEADS * HEAD_SIZE), 1.0, 6.0, ((0, 16), (1, 2))),
        "leaf_key_block": noise(splits[3], (N_TOK * LEAF_BLOCK_ROWS, KEY_VALUE_HEADS * HEAD_SIZE), 1.0, 6.0, ((0, 16), (1, 2))),
        "leaf_value_block": noise(splits[4], (N_TOK * LEAF_BLOCK_ROWS, KEY_VALUE_HEADS * HEAD_SIZE), 1.0, 6.0, ((0, 16), (1, 2))),
        "shared_key_block": noise(splits[5], (N_TOK * NODE_ROW_LIMIT, KEY_VALUE_HEADS * HEAD_SIZE), 1.0, 6.0, ((0, 16), (1, 2))),
        "shared_value_block": noise(splits[6], (N_TOK * NODE_ROW_LIMIT, KEY_VALUE_HEADS * HEAD_SIZE), 1.0, 6.0, ((0, 16), (1, 2))),
        "out_weight": noise(splits[7], (HQ * HEAD_SIZE, D), (HQ * HEAD_SIZE) ** -0.5, 0.0625, ((0, 2), (1, 16))),
        "residual": noise(splits[8], (PACKED_TOKENS, D), 0.3, 2.5, ((0, 2), (1, 16))),
        "token_request": draw_token_request(jax.random.fold_in(splits[14], 71), 0),
        "positions": draw_positions(jax.random.fold_in(splits[14], 71), 0),
        "parents": draw_parents(jax.random.fold_in(splits[14], 71), 0),
        "node_lengths": draw_node_lengths(jax.random.fold_in(splits[14], 71), 0),
        "node_owner": draw_node_owner(jax.random.fold_in(splits[14], 71), 0),
    }


THETA = 5000000.0
NEG = -1e+30

def apply_rotary(values, position, heads):
    width = values.shape[1] // heads
    half = width // 2
    table = values.astype(jnp.float32).reshape(values.shape[0], heads, width)
    freq = THETA ** (-(jnp.arange(half, dtype=jnp.float32) * 2.0) / width)
    angle = position.astype(jnp.float32)[:, None] * freq[None, :]
    cosine = jnp.cos(angle)[:, None, :]
    sine = jnp.sin(angle)[:, None, :]
    first = table[:, :, :half]
    second = table[:, :, half:]
    turned = jnp.concatenate([first * cosine - second * sine, second * cosine + first * sine], axis=2)
    return turned.reshape(values.shape).astype(jnp.bfloat16)

def attend_key_block(queries4, keys, values, valid):
    scale = 1.0 / math.sqrt(queries4.shape[-1])
    scores = jnp.einsum('sgqd,rgd->sgqr', queries4.astype(jnp.float32), keys.astype(jnp.float32)) * scale
    allowed = valid[:, None, None, :]
    highest = lax.optimization_barrier(jnp.max(jnp.where(allowed, scores, NEG), axis=3))
    weights = jnp.where(allowed, jnp.exp(scores - highest[..., None]), 0.0).astype(jnp.bfloat16)
    total = lax.optimization_barrier(jnp.sum(weights.astype(jnp.float32), axis=3))
    output = jnp.einsum('sgqr,rgd->sgqd', weights.astype(jnp.float32), values.astype(jnp.float32))
    return (highest, total, output)

def reference(queries, fresh_token_keys, fresh_token_values, leaf_key_block, leaf_value_block, shared_key_block, shared_value_block, out_weight, residual, token_request, positions, parents, node_lengths, node_owner):
    query_turned = apply_rotary(queries, positions, HQ)
    key_turned = apply_rotary(fresh_token_keys, positions, KEY_VALUE_HEADS)
    order = jnp.argsort(token_request, stable=True).astype(jnp.int32).reshape(REQUEST_COUNT, REQUEST_TOKENS)
    leaf_owner = node_owner[ROOTS + MIDS:]
    row_ids = jnp.arange(LEAF_BLOCK_ROWS, dtype=jnp.int32)
    node_row_ids = jnp.arange(NODE_ROW_LIMIT, dtype=jnp.int32)

    def one_request(request):
        token_positions = order[request]
        leaf = ROOTS + MIDS + request
        middle = parents[leaf]
        root = parents[middle]
        leaf_length = node_lengths[leaf]
        new_index = positions[token_positions] - node_lengths[root] - node_lengths[middle] - leaf_length
        owner = leaf_owner[request]
        slab_keys = lax.dynamic_slice_in_dim(leaf_key_block, (owner * LEAF_BLOCK_ROWS).astype(jnp.int32), LEAF_BLOCK_ROWS, 0)
        slab_values = lax.dynamic_slice_in_dim(leaf_value_block, (owner * LEAF_BLOCK_ROWS).astype(jnp.int32), LEAF_BLOCK_ROWS, 0)
        place = (row_ids[:, None] == (leaf_length + new_index)[None, :]).astype(jnp.bfloat16)
        put_keys = jnp.dot(place, key_turned[token_positions], preferred_element_type=jnp.float32).astype(jnp.bfloat16)
        put_values = jnp.dot(place, fresh_token_values[token_positions], preferred_element_type=jnp.float32).astype(jnp.bfloat16)
        keep = row_ids[:, None] < leaf_length
        written_keys = jnp.where(keep, slab_keys, put_keys)
        written_values = jnp.where(keep, slab_values, put_values)
        shared_key_rows = []
        shared_value_rows = []
        shared_ok = []
        for node in (root, middle):
            first = (node_owner[node] * NODE_ROW_LIMIT).astype(jnp.int32)
            shared_key_rows.append(lax.dynamic_slice_in_dim(shared_key_block, first, NODE_ROW_LIMIT, 0))
            shared_value_rows.append(lax.dynamic_slice_in_dim(shared_value_block, first, NODE_ROW_LIMIT, 0))
            shared_ok.append(node_row_ids < node_lengths[node])
        joined_keys = jnp.concatenate(shared_key_rows, axis=0).reshape(2 * NODE_ROW_LIMIT, KEY_VALUE_HEADS, HEAD_SIZE)
        joined_values = jnp.concatenate(shared_value_rows, axis=0).reshape(2 * NODE_ROW_LIMIT, KEY_VALUE_HEADS, HEAD_SIZE)
        valid_both = jnp.concatenate(shared_ok, axis=0)
        grouped_queries = query_turned[token_positions].reshape(REQUEST_TOKENS, KEY_VALUE_HEADS, QUERY_PER_GROUP, HEAD_SIZE)
        high_a, total_a, out_a = attend_key_block(grouped_queries, joined_keys, joined_values, valid_both[None, :])
        leaf_row_mask = row_ids[None, :] < (leaf_length + new_index + 1)[:, None]
        running_peak_b, running_sum_b, partial_output_b = attend_key_block(grouped_queries, written_keys.reshape(LEAF_BLOCK_ROWS, KEY_VALUE_HEADS, HEAD_SIZE), written_values.reshape(LEAF_BLOCK_ROWS, KEY_VALUE_HEADS, HEAD_SIZE), leaf_row_mask)
        highest = jnp.maximum(high_a, running_peak_b)
        scale_a = jnp.exp(high_a - highest)
        scale_b = jnp.exp(running_peak_b - highest)
        merged = (scale_a[..., None] * out_a + scale_b[..., None] * partial_output_b) / (scale_a * total_a + scale_b * running_sum_b)[..., None]
        return (merged.reshape(REQUEST_TOKENS, HQ * HEAD_SIZE).astype(jnp.bfloat16), written_keys, written_values)
    attended_req, request_keys, request_values = lax.map(one_request, jnp.arange(REQUEST_COUNT, dtype=jnp.int32))
    inverse_frequency = jnp.argsort(leaf_owner).astype(jnp.int32)
    leaf_key_output = request_keys[inverse_frequency].reshape(REQUEST_COUNT * LEAF_BLOCK_ROWS, KEY_VALUE_HEADS * HEAD_SIZE)
    leaf_value_output = request_values[inverse_frequency].reshape(REQUEST_COUNT * LEAF_BLOCK_ROWS, KEY_VALUE_HEADS * HEAD_SIZE)
    attended = jnp.zeros((PACKED_TOKENS, HQ * HEAD_SIZE), jnp.bfloat16).at[order.reshape(-1)].set(attended_req.reshape(PACKED_TOKENS, HQ * HEAD_SIZE))
    projected = jnp.dot(attended, out_weight, preferred_element_type=jnp.float32)
    hidden = (residual.astype(jnp.float32) + projected).astype(jnp.bfloat16)
    return (hidden, leaf_key_output, leaf_value_output)
```

```python
import functools
import math

import jax
import jax.numpy as jnp
import numpy as np
from jax import lax
from jax.experimental import pallas as pl
from jax.experimental.pallas import tpu as pltpu
from jax.sharding import PartitionSpec as P

HEAD_SIZE = 128
ROOTS = 2
MIDS = 8
THETA = 5000000.0
NEG = -1e30
LEVELS = 4
ORDER = ((0, 1, 2, 3), (1, 0, 2, 3), (2, 3, 1, 0), (3, 2, 1, 0))
MESH = pl.DeviceIdType.MESH


def kernel(
    N, M,
    queries, fresh_k, fresh_v, leaf_k, leaf_v, shared_k, shared_v, weight, residual,
    freq, request, pos, parents, lengths, owners,
    hidden, leaf_k_out, leaf_v_out,
    kv, att, w, qrot, own_acc, sums, out_sums, in_sums,
    kv_recv, kv_up, kv_down, kv_side, kv_core,
    at_recv, at_up, at_down, at_side, at_core,
    sum_send, sum_recv, local,
):
    t = lax.axis_index("tok")
    y = lax.axis_index("mlp")
    B = N // (2 * LEVELS)
    a, b, c = t // (2 * B), (t // 2) % B, t % 2
    rows = queries.shape[0]
    heads = kv.shape[3] // HEAD_SIZE
    group = queries.shape[1] // HEAD_SIZE // heads
    gw = group * HEAD_SIZE

    def tid(a_, b_, c_):
        return (a_ * B + b_) * 2 + c_

    def level(k):
        code = sum(ORDER[i][k] * 4**i for i in range(LEVELS))
        return (code // jnp.where(a == 0, 1, jnp.where(a == 1, 4, jnp.where(a == 2, 16, 64)))) % 4

    barrier = pltpu.get_barrier_semaphore()

    def greet(dev):
        pl.semaphore_signal(barrier, inc=1, device_id=dev, device_id_type=MESH)

    @pl.when(a > 0)
    def _():
        greet((tid(a - 1, b, c), y))

    @pl.when(a < LEVELS - 1)
    def _():
        greet((tid(a + 1, b, c), y))

    for j in range(1, B):
        greet((tid(a, (b + j) % B, c), y))
    greet((tid(a, b, 1 - c), y))
    for j in range(1, M):
        greet((t, (y + j) % M))

    loads = [
        pltpu.make_async_copy(shared_k, kv.at[0, t], local.at[0]),
        pltpu.make_async_copy(shared_v, kv.at[1, t], local.at[1]),
        pltpu.make_async_copy(weight, w, local.at[2]),
    ]
    for load in loads:
        load.start()
    pl.semaphore_wait(
        barrier, B + M - 1 + jnp.minimum(a, 1) + jnp.minimum(LEVELS - 1 - a, 1)
    )

    def copy(src, dst, ss, rs, dev):
        return pltpu.make_async_remote_copy(
            src_ref=src, dst_ref=dst, send_sem=ss, recv_sem=rs,
            device_id=(dev, y), device_id_type=MESH,
        )

    def stage1(buf, recv, up, down, side, core, k, it, src=None, go=True):
        L = level(k)
        slot = tid(L, b, c)
        dst = buf.at[it, slot]
        rs = recv.at[it, slot]
        if go and k > 0:
            copy(dst, dst, core.at[k, it, 0], rs, tid(a, b, 1 - c)).wait_recv()
        src = dst if src is None else src
        act = (lambda d: d.start()) if go else (lambda d: d.wait_send())

        @pl.when(jnp.logical_and(L <= a, a < LEVELS - 1))
        def _():
            act(copy(src, dst, up.at[k, it], rs, tid(a + 1, b, c)))

        @pl.when(jnp.logical_and(L >= a, a > 0))
        def _():
            act(copy(src, dst, down.at[k, it], rs, tid(a - 1, b, c)))

        for j in range(1, B):
            act(copy(src, dst, side.at[k, it, j - 1], rs, tid(a, (b + j) % B, c)))
        act(copy(src, dst, core.at[k, it, 0], rs, tid(a, b, 1 - c)))

    def stage2(buf, recv, up, down, side, core, k, it, go=True):
        L = level(k)
        for j in range(1, B):
            slot = tid(L, (b + j) % B, c)
            d = copy(
                buf.at[it, slot], buf.at[it, slot], core.at[k, it, j],
                recv.at[it, slot], tid(a, b, 1 - c),
            )
            if go:
                d.wait_recv()
                d.start()
            else:
                d.wait_send()

    def stage3(buf, recv, up, down, side, core, k, it):
        L = level(k)
        for j in range(B):
            slot = tid(L, (b + j) % B, 1 - c)
            copy(
                buf.at[it, slot], buf.at[it, slot], core.at[k, it, j],
                recv.at[it, slot], tid(a, b, 1 - c),
            ).wait_recv()

    kvs = (kv, kv_recv, kv_up, kv_down, kv_side, kv_core)
    ats = (att, at_recv, at_up, at_down, at_side, at_core)
    own = (shared_k, shared_v)

    stage1(*kvs, 0, 0, shared_k)
    stage1(*kvs, 0, 1, shared_v)

    leaf = ROOTS + MIDS + request[t * rows]
    middle = parents[leaf]
    root = parents[middle]
    leaf_length = lengths[leaf]
    root_length = lengths[root]
    middle_length = lengths[middle]
    prefix = root_length + middle_length
    eye = lax.broadcasted_iota(jnp.int32, (rows, rows), 0) == lax.broadcasted_iota(
        jnp.int32, (rows, rows), 1
    )
    pos_row = pos[...]
    pos_column = jnp.sum(
        jnp.where(eye, pos_row.astype(jnp.float32), 0.0), axis=1, keepdims=True
    )
    angle = pos_column * freq[...]
    cosine = jnp.cos(angle)
    lane = lax.broadcasted_iota(jnp.int32, (rows, HEAD_SIZE), 1)
    sine = jnp.where(lane < HEAD_SIZE // 2, -1.0, 1.0) * jnp.sin(angle)

    def turn(block):
        block = block.astype(jnp.float32)
        return (block * cosine + pltpu.roll(block, HEAD_SIZE // 2, 1) * sine).astype(jnp.bfloat16)

    for g in range(heads):
        for h in range(group):
            at = (g * group + h) * HEAD_SIZE
            qrot[g, h * rows : (h + 1) * rows, :] = turn(queries[:, at : at + HEAD_SIZE])

    leaf_rows = leaf_k.shape[0]
    row_ids = lax.broadcasted_iota(jnp.int32, (leaf_rows, rows), 0)
    place = jnp.where(row_ids == pos_row - prefix, 1.0, 0.0).astype(jnp.bfloat16)
    keep = lax.broadcasted_iota(jnp.int32, (leaf_rows, HEAD_SIZE), 0) < leaf_length
    for g in range(heads):
        s = slice(g * HEAD_SIZE, (g + 1) * HEAD_SIZE)
        pair = jnp.concatenate([turn(fresh_k[:, s]), fresh_v[:, s]], axis=1)
        put = jnp.dot(place, pair, preferred_element_type=jnp.float32)
        leaf_k_out[:, s] = jnp.where(
            keep, leaf_k[:, s].astype(jnp.float32), put[:, :HEAD_SIZE]
        ).astype(jnp.bfloat16)
        leaf_v_out[:, s] = jnp.where(
            keep, leaf_v[:, s].astype(jnp.float32), put[:, HEAD_SIZE:]
        ).astype(jnp.bfloat16)

    items = [(k, it) for k in range(LEVELS) for it in range(2)]
    for i in range(2, len(items) + 1):
        if i < len(items):
            stage1(*kvs, *items[i])
        if i == 2:
            stage2(*kvs, *items[0])
        stage2(*kvs, *items[i - 1])
    for item in items:
        stage3(*kvs, *item)
    loads[0].wait()
    loads[1].wait()

    node_rows = shared_k.shape[0]
    root_owner = owners[root]
    middle_owner = owners[middle]
    node_ids = lax.broadcasted_iota(jnp.int32, (1, node_rows), 1)
    shared_bias = jnp.concatenate(
        [
            jnp.where(node_ids < root_length, 0.0, NEG),
            jnp.where(node_ids < middle_length, 0.0, NEG),
        ],
        axis=1,
    )
    limit = jnp.concatenate([pos_column - (prefix - 1).astype(jnp.float32)] * group, axis=0)
    leaf_ids = lax.broadcasted_iota(jnp.int32, (1, leaf_rows), 1).astype(jnp.float32)
    factor = math.log2(math.e) / math.sqrt(HEAD_SIZE)
    ones = jnp.ones((2 * node_rows + leaf_rows, HEAD_SIZE), jnp.bfloat16)
    contract = (((1,), (1,)), ((), ()))

    def attend(g):
        s = slice(g * HEAD_SIZE, (g + 1) * HEAD_SIZE)
        q = qrot[g]
        shared_keys = jnp.concatenate([kv[0, root_owner, :, s], kv[0, middle_owner, :, s]], axis=0)
        values = jnp.concatenate(
            [kv[1, root_owner, :, s], kv[1, middle_owner, :, s], leaf_v_out[:, s]], axis=0
        )
        s1 = lax.dot_general(q, shared_keys, contract, preferred_element_type=jnp.float32)
        s2 = lax.dot_general(q, leaf_k_out[:, s], contract, preferred_element_type=jnp.float32)
        s1 = s1 + shared_bias
        s2 = jnp.where(leaf_ids < limit, s2, NEG)
        highest = jnp.maximum(
            jnp.max(s1, axis=1, keepdims=True), jnp.max(s2, axis=1, keepdims=True)
        )
        p = jnp.concatenate(
            [
                jnp.exp2((s1 - highest) * factor).astype(jnp.bfloat16),
                jnp.exp2((s2 - highest) * factor).astype(jnp.bfloat16),
            ],
            axis=1,
        )
        o = jnp.dot(
            p, jnp.concatenate([values, ones], axis=1), preferred_element_type=jnp.float32
        )
        o = (o[:, :HEAD_SIZE] / o[:, HEAD_SIZE:]).astype(jnp.bfloat16)
        for h in range(group):
            att[g, t, :, h * HEAD_SIZE : (h + 1) * HEAD_SIZE] = o[h * rows : (h + 1) * rows, :]

    for g in range(heads):
        attend(g)
        stage1(*ats, 0, g)

    loads[2].wait()
    pieces = N // 4
    per_level = pieces // LEVELS
    share = pieces // M

    def piece(k, i):
        return level(k) * per_level + i

    def sum_copy(k, i):
        p = piece(k, i)
        return pltpu.make_async_remote_copy(
            src_ref=out_sums.at[k * per_level + i], dst_ref=in_sums.at[y, p % share],
            send_sem=sum_send.at[k * per_level + i], recv_sem=sum_recv.at[y, p % share],
            device_id=(t, p // share), device_id_type=MESH,
        )

    def project(k, g):
        for i in range(per_level):
            p = piece(k, i)
            block = att[g, pl.ds(p * 4, 4)].reshape(4 * rows, gw)
            part = jnp.dot(
                block, w[g * gw : (g + 1) * gw, :], preferred_element_type=jnp.float32
            )
            if g > 0:
                part = sums[i] + part
            if g < heads - 1:
                sums[i] = part
                continue

            @pl.when(p // share == y)
            def _():
                own_acc[p % share] = part

            @pl.when(p // share != y)
            def _():
                out_sums[k * per_level + i] = part.astype(jnp.bfloat16)
                sum_copy(k, i).start()

    items = [(k, g) for k in range(LEVELS) for g in range(heads)]
    n = len(items)
    for i in range(n + 3):
        if heads <= i < n:
            stage1(*ats, *items[i])
        if 0 <= i - 1 < n:
            stage2(*ats, *items[i - 1])
        if 0 <= i - 3 < n:
            stage3(*ats, *items[i - 3])
            project(*items[i - 3])

    total = residual[...].astype(jnp.float32) + own_acc[...].reshape(residual.shape)
    for j in range(1, M):
        other = (y + j) % M
        for r in range(share):
            pltpu.make_async_remote_copy(
                src_ref=in_sums.at[other, r], dst_ref=in_sums.at[other, r],
                send_sem=sum_send.at[0], recv_sem=sum_recv.at[other, r],
                device_id=(t, other), device_id_type=MESH,
            ).wait_recv()
        total = total + in_sums[other].astype(jnp.float32).reshape(residual.shape)
    hidden[...] = total.astype(jnp.bfloat16)

    for k in range(LEVELS):
        for it in range(2):
            stage1(*kvs, k, it, own[it] if k == 0 else None, go=False)
            stage2(*kvs, k, it, go=False)
        for g in range(heads):
            stage1(*ats, k, g, go=False)
            stage2(*ats, k, g, go=False)
        for i in range(per_level):

            @pl.when(piece(k, i) // share != y)
            def _():
                sum_copy(k, i).wait_send()


def body(
    N, M,
    queries, fresh_k, fresh_v, leaf_k, leaf_v, shared_k, shared_v, weight, residual,
    request, positions, parents, lengths, owners,
):
    rows, q_width = queries.shape
    kv_width = fresh_k.shape[1]
    heads = kv_width // HEAD_SIZE
    group = q_width // kv_width
    half = HEAD_SIZE // 2
    B = N // (2 * LEVELS)
    columns = weight.shape[1]
    pieces = N // 4
    per_level = pieces // LEVELS
    share = pieces // M
    exponent = np.tile(np.arange(half, dtype=np.float64) * 2.0 / HEAD_SIZE, 2)
    freq = jnp.asarray((THETA**-exponent)[None, :].astype(np.float32))
    vmem = pl.BlockSpec(memory_space=pltpu.VMEM)
    anywhere = pl.BlockSpec(memory_space=pl.ANY)
    smem = pl.BlockSpec(memory_space=pltpu.SMEM)
    dma = pltpu.SemaphoreType.DMA
    bf16, f32 = jnp.bfloat16, jnp.float32

    def semaphores(items):
        return [
            dma((items, N)), dma((LEVELS, items)), dma((LEVELS, items)),
            dma((LEVELS, items, B - 1)), dma((LEVELS, items, B)),
        ]

    return pl.pallas_call(
        functools.partial(kernel, N, M),
        out_shape=(
            jax.ShapeDtypeStruct(residual.shape, bf16),
            jax.ShapeDtypeStruct(leaf_k.shape, bf16),
            jax.ShapeDtypeStruct(leaf_v.shape, bf16),
        ),
        in_specs=[vmem] * 5 + [anywhere] * 3 + [vmem] * 2 + [smem, vmem] + [smem] * 3,
        out_specs=(vmem, vmem, vmem),
        scratch_shapes=[
            pltpu.VMEM((2, N) + shared_k.shape, bf16),
            pltpu.VMEM((heads, N, rows, group * HEAD_SIZE), bf16),
            pltpu.VMEM(weight.shape, bf16),
            pltpu.VMEM((heads, group * rows, HEAD_SIZE), bf16),
            pltpu.VMEM((share, 4 * rows, columns), f32),
            pltpu.VMEM((per_level, 4 * rows, columns), f32),
            pltpu.VMEM((pieces, 4 * rows, columns), bf16),
            pltpu.VMEM((M, share, 4 * rows, columns), bf16),
        ]
        + semaphores(2)
        + semaphores(heads)
        + [dma((pieces,)), dma((M, share)), dma((3,))],
        compiler_params=pltpu.CompilerParams(
            collective_id=0, has_side_effects=True, vmem_limit_bytes=56 * 1024 * 1024
        ),
    )(
        queries, fresh_k, fresh_v, leaf_k, leaf_v, shared_k, shared_v, weight, residual,
        freq, request, positions.reshape(1, rows), parents, lengths, owners,
    )


def solution(mesh):
    both = P("tok", "mlp")
    return jax.shard_map(
        functools.partial(body, mesh.shape["tok"], mesh.shape["mlp"]),
        mesh=mesh,
        in_specs=(both,) * 7 + (P("mlp", "tok"),) * 2 + (P(), P("tok"), P(), P(), P()),
        out_specs=(P("mlp", "tok"), both, both),
        check_vma=False,
    )
```

```python
import functools
import math

import jax
import jax.numpy as jnp
import numpy as np
from jax import lax
from jax.experimental import pallas as pl
from jax.experimental.pallas import tpu as pltpu
from jax.sharding import PartitionSpec as P

HEAD_SIZE = 128
ROOTS = 2
MIDS = 8
THETA = 5000000.0
NEG = -1e30
LEVELS = 4
ORDER = ((0, 1, 2, 3), (1, 0, 2, 3), (2, 3, 1, 0), (3, 2, 1, 0))
MESH = pl.DeviceIdType.MESH


def kernel(
    N, M,
    queries, fresh_k, fresh_v, leaf_k, leaf_v, shared_k, shared_v, weight, residual,
    freq, request, pos, parents, lengths, owners,
    hidden, leaf_k_out, leaf_v_out,
    kv, att, w, qrot, own_acc, sums, out_sums, in_sums,
    kv_recv, kv_up, kv_down, kv_side, kv_core, kv_cross,
    at_recv, at_up, at_down, at_side, at_core, at_cross,
    sum_send, sum_recv, local,
):
    t = lax.axis_index("tok")
    y = lax.axis_index("mlp")
    B = N // (2 * LEVELS)
    a, b, c = t // (2 * B), (t // 2) % B, t % 2
    rows = queries.shape[0]
    heads = kv.shape[3] // HEAD_SIZE
    group = queries.shape[1] // HEAD_SIZE // heads
    gw = group * HEAD_SIZE

    def tid(a_, b_, c_):
        return (a_ * B + b_) * 2 + c_

    def level(k):
        code = sum(ORDER[i][k] * 4**i for i in range(LEVELS))
        return (code // jnp.where(a == 0, 1, jnp.where(a == 1, 4, jnp.where(a == 2, 16, 64)))) % 4

    barrier = pltpu.get_barrier_semaphore()

    def greet(dev):
        pl.semaphore_signal(barrier, inc=1, device_id=dev, device_id_type=MESH)

    @pl.when(a > 0)
    def _():
        greet((tid(a - 1, b, c), y))

    @pl.when(a < LEVELS - 1)
    def _():
        greet((tid(a + 1, b, c), y))

    for j in range(1, B):
        greet((tid(a, (b + j) % B, c), y))
    greet((tid(a, b, 1 - c), y))
    for j in range(1, M):
        greet((t, (y + j) % M))

    loads = [
        pltpu.make_async_copy(shared_k, kv.at[0, t], local.at[0]),
        pltpu.make_async_copy(shared_v, kv.at[1, t], local.at[1]),
        pltpu.make_async_copy(weight, w, local.at[2]),
    ]
    for load in loads:
        load.start()
    pl.semaphore_wait(
        barrier, B + M - 1 + jnp.minimum(a, 1) + jnp.minimum(LEVELS - 1 - a, 1)
    )

    def copy(src, dst, ss, rs, dev):
        return pltpu.make_async_remote_copy(
            src_ref=src, dst_ref=dst, send_sem=ss, recv_sem=rs,
            device_id=(dev, y), device_id_type=MESH,
        )

    def far(buf, it):
        return B == 2 and it >= buf.shape[0] // 2

    def stage1(buf, recv, up, down, side, core, cross, k, it, src=None, go=True):
        L = level(k)
        slot = tid(L, b, c)
        dst = buf.at[it, slot]
        rs = recv.at[it, slot]
        if go and k > 0:
            copy(dst, dst, core.at[k, it, 0], rs, tid(a, b, 1 - c)).wait_recv()
        src = dst if src is None else src
        act = (lambda d: d.start()) if go else (lambda d: d.wait_send())

        @pl.when(jnp.logical_and(L <= a, a < LEVELS - 1))
        def _():
            act(copy(src, dst, up.at[k, it], rs, tid(a + 1, b, c)))

        @pl.when(jnp.logical_and(L >= a, a > 0))
        def _():
            act(copy(src, dst, down.at[k, it], rs, tid(a - 1, b, c)))

        act(copy(src, dst, core.at[k, it, 0], rs, tid(a, b, 1 - c)))

        def to_sides():
            for j in range(1, B):
                act(copy(src, dst, side.at[k, it, j - 1], rs, tid(a, (b + j) % B, c)))

        if k > 0 and far(buf, it):
            pl.when(L % (LEVELS - 1) != 0)(to_sides)
        else:
            to_sides()

    def stage2(buf, recv, up, down, side, core, cross, k, it, go=True):
        L = level(k)
        for j in range(1, B):
            slot = tid(L, (b + j) % B, c)
            d = copy(
                buf.at[it, slot], buf.at[it, slot], core.at[k, it, j],
                recv.at[it, slot], tid(a, b, 1 - c),
            )
            if go:
                d.wait_recv()
                d.start()
            else:
                d.wait_send()
            if far(buf, it):
                for end, ahead, step in ((0, a < LEVELS - 1, 1), (LEVELS - 1, a > 0, -1)):

                    @pl.when(jnp.logical_and(L == end, ahead))
                    def _():
                        onward = copy(
                            buf.at[it, slot], buf.at[it, slot], cross.at[k, it],
                            recv.at[it, slot], tid(a + step, b, c),
                        )
                        if go:
                            onward.start()
                        else:
                            onward.wait_send()

    def stage3(buf, recv, up, down, side, core, cross, k, it):
        L = level(k)
        for j in range(B):
            slot = tid(L, (b + j) % B, 1 - c)
            copy(
                buf.at[it, slot], buf.at[it, slot], core.at[k, it, j],
                recv.at[it, slot], tid(a, b, 1 - c),
            ).wait_recv()

    kvs = (kv, kv_recv, kv_up, kv_down, kv_side, kv_core, kv_cross)
    ats = (att, at_recv, at_up, at_down, at_side, at_core, at_cross)
    own = (shared_k, shared_v)

    stage1(*kvs, 0, 0, shared_k)
    stage1(*kvs, 0, 1, shared_v)

    leaf = ROOTS + MIDS + request[t * rows]
    middle = parents[leaf]
    root = parents[middle]
    leaf_length = lengths[leaf]
    root_length = lengths[root]
    middle_length = lengths[middle]
    prefix = root_length + middle_length
    eye = lax.broadcasted_iota(jnp.int32, (rows, rows), 0) == lax.broadcasted_iota(
        jnp.int32, (rows, rows), 1
    )
    pos_row = pos[...]
    pos_column = jnp.sum(
        jnp.where(eye, pos_row.astype(jnp.float32), 0.0), axis=1, keepdims=True
    )
    angle = pos_column * freq[...]
    cosine = jnp.cos(angle)
    lane = lax.broadcasted_iota(jnp.int32, (rows, HEAD_SIZE), 1)
    sine = jnp.where(lane < HEAD_SIZE // 2, -1.0, 1.0) * jnp.sin(angle)

    def turn(block):
        block = block.astype(jnp.float32)
        return (block * cosine + pltpu.roll(block, HEAD_SIZE // 2, 1) * sine).astype(jnp.bfloat16)

    for g in range(heads):
        for h in range(group):
            at = (g * group + h) * HEAD_SIZE
            qrot[g, h * rows : (h + 1) * rows, :] = turn(queries[:, at : at + HEAD_SIZE])

    leaf_rows = leaf_k.shape[0]
    row_ids = lax.broadcasted_iota(jnp.int32, (leaf_rows, rows), 0)
    place = jnp.where(row_ids == pos_row - prefix, 1.0, 0.0).astype(jnp.bfloat16)
    keep = lax.broadcasted_iota(jnp.int32, (leaf_rows, HEAD_SIZE), 0) < leaf_length
    for g in range(heads):
        s = slice(g * HEAD_SIZE, (g + 1) * HEAD_SIZE)
        pair = jnp.concatenate([turn(fresh_k[:, s]), fresh_v[:, s]], axis=1)
        put = jnp.dot(place, pair, preferred_element_type=jnp.float32)
        leaf_k_out[:, s] = jnp.where(
            keep, leaf_k[:, s].astype(jnp.float32), put[:, :HEAD_SIZE]
        ).astype(jnp.bfloat16)
        leaf_v_out[:, s] = jnp.where(
            keep, leaf_v[:, s].astype(jnp.float32), put[:, HEAD_SIZE:]
        ).astype(jnp.bfloat16)

    items = [(k, it) for k in range(LEVELS) for it in range(2)]
    for i in range(2, len(items) + 1):
        if i < len(items):
            stage1(*kvs, *items[i])
        if i == 2:
            stage2(*kvs, *items[0])
        stage2(*kvs, *items[i - 1])
    for item in items:
        stage3(*kvs, *item)
    loads[0].wait()
    loads[1].wait()

    node_rows = shared_k.shape[0]
    root_owner = owners[root]
    middle_owner = owners[middle]
    node_ids = lax.broadcasted_iota(jnp.int32, (1, node_rows), 1)
    shared_bias = jnp.concatenate(
        [
            jnp.where(node_ids < root_length, 0.0, NEG),
            jnp.where(node_ids < middle_length, 0.0, NEG),
        ],
        axis=1,
    )
    limit = jnp.concatenate([pos_column - (prefix - 1).astype(jnp.float32)] * group, axis=0)
    leaf_ids = lax.broadcasted_iota(jnp.int32, (1, leaf_rows), 1).astype(jnp.float32)
    factor = math.log2(math.e) / math.sqrt(HEAD_SIZE)
    ones = jnp.ones((2 * node_rows + leaf_rows, HEAD_SIZE), jnp.bfloat16)
    contract = (((1,), (1,)), ((), ()))

    def attend(g):
        s = slice(g * HEAD_SIZE, (g + 1) * HEAD_SIZE)
        q = qrot[g]
        shared_keys = jnp.concatenate([kv[0, root_owner, :, s], kv[0, middle_owner, :, s]], axis=0)
        values = jnp.concatenate(
            [kv[1, root_owner, :, s], kv[1, middle_owner, :, s], leaf_v_out[:, s]], axis=0
        )
        s1 = lax.dot_general(q, shared_keys, contract, preferred_element_type=jnp.float32)
        s2 = lax.dot_general(q, leaf_k_out[:, s], contract, preferred_element_type=jnp.float32)
        s1 = s1 + shared_bias
        s2 = jnp.where(leaf_ids < limit, s2, NEG)
        highest = jnp.maximum(
            jnp.max(s1, axis=1, keepdims=True), jnp.max(s2, axis=1, keepdims=True)
        )
        p = jnp.concatenate(
            [
                jnp.exp2((s1 - highest) * factor).astype(jnp.bfloat16),
                jnp.exp2((s2 - highest) * factor).astype(jnp.bfloat16),
            ],
            axis=1,
        )
        o = jnp.dot(
            p, jnp.concatenate([values, ones], axis=1), preferred_element_type=jnp.float32
        )
        o = (o[:, :HEAD_SIZE] / o[:, HEAD_SIZE:]).astype(jnp.bfloat16)
        for h in range(group):
            att[g, t, :, h * HEAD_SIZE : (h + 1) * HEAD_SIZE] = o[h * rows : (h + 1) * rows, :]

    for g in range(heads):
        attend(g)
        stage1(*ats, 0, g)

    loads[2].wait()
    pieces = N // 4
    per_level = pieces // LEVELS
    share = pieces // M

    def piece(k, i):
        return level(k) * per_level + i

    def sum_copy(k, i):
        p = piece(k, i)
        return pltpu.make_async_remote_copy(
            src_ref=out_sums.at[k * per_level + i], dst_ref=in_sums.at[y, p % share],
            send_sem=sum_send.at[k * per_level + i], recv_sem=sum_recv.at[y, p % share],
            device_id=(t, p // share), device_id_type=MESH,
        )

    def project(k, g):
        for i in range(per_level):
            p = piece(k, i)
            block = att[g, pl.ds(p * 4, 4)].reshape(4 * rows, gw)
            part = lax.dot_general(
                w[:, g * gw : (g + 1) * gw], block, contract, preferred_element_type=jnp.float32
            )
            if g > 0:
                part = sums[i] + part
            if g < heads - 1:
                sums[i] = part
                continue

            @pl.when(p // share == y)
            def _():
                own_acc[p % share] = part

            @pl.when(p // share != y)
            def _():
                out_sums[k * per_level + i] = part.astype(jnp.bfloat16)
                sum_copy(k, i).start()

    items = [(k, g) for k in range(LEVELS) for g in range(heads)]
    n = len(items)
    for i in range(n + 3):
        if heads <= i < n:
            stage1(*ats, *items[i])
        if 0 <= i - 1 < n:
            stage2(*ats, *items[i - 1])
        if 0 <= i - 3 < n:
            stage3(*ats, *items[i - 3])
            project(*items[i - 3])

    def across(sums_of):
        return jnp.concatenate([sums_of(r).astype(jnp.float32) for r in range(share)], axis=1)

    total = residual[...].astype(jnp.float32) + across(lambda r: own_acc[r])
    for j in range(1, M):
        other = (y + j) % M
        for r in range(share):
            pltpu.make_async_remote_copy(
                src_ref=in_sums.at[other, r], dst_ref=in_sums.at[other, r],
                send_sem=sum_send.at[0], recv_sem=sum_recv.at[other, r],
                device_id=(t, other), device_id_type=MESH,
            ).wait_recv()
        total = total + across(lambda r: in_sums[other, r])
    hidden[...] = total.astype(jnp.bfloat16)

    for k in range(LEVELS):
        for it in range(2):
            stage1(*kvs, k, it, own[it] if k == 0 else None, go=False)
            stage2(*kvs, k, it, go=False)
        for g in range(heads):
            stage1(*ats, k, g, go=False)
            stage2(*ats, k, g, go=False)
        for i in range(per_level):

            @pl.when(piece(k, i) // share != y)
            def _():
                sum_copy(k, i).wait_send()


def hand_over(*refs):
    for source, target in zip(refs[:3], refs[3:]):
        target[...] = source[...]


def body(
    N, M,
    queries, fresh_k, fresh_v, leaf_k, leaf_v, shared_k, shared_v, weight, residual,
    request, positions, parents, lengths, owners,
):
    rows, q_width = queries.shape
    kv_width = fresh_k.shape[1]
    heads = kv_width // HEAD_SIZE
    group = q_width // kv_width
    half = HEAD_SIZE // 2
    B = N // (2 * LEVELS)
    weight, residual = weight.T, residual.T
    columns = weight.shape[0]
    pieces = N // 4
    per_level = pieces // LEVELS
    share = pieces // M
    exponent = np.tile(np.arange(half, dtype=np.float64) * 2.0 / HEAD_SIZE, 2)
    freq = jnp.asarray((THETA**-exponent)[None, :].astype(np.float32))
    vmem = pl.BlockSpec(memory_space=pltpu.VMEM)
    anywhere = pl.BlockSpec(memory_space=pl.ANY)
    smem = pl.BlockSpec(memory_space=pltpu.SMEM)
    dma = pltpu.SemaphoreType.DMA
    bf16, f32 = jnp.bfloat16, jnp.float32

    def semaphores(items):
        return [
            dma((items, N)), dma((LEVELS, items)), dma((LEVELS, items)),
            dma((LEVELS, items, B - 1)), dma((LEVELS, items, B)), dma((LEVELS, items)),
        ]

    hidden, leaf_k_out, leaf_v_out = pl.pallas_call(
        functools.partial(kernel, N, M),
        out_shape=(
            jax.ShapeDtypeStruct(residual.shape, bf16),
            jax.ShapeDtypeStruct(leaf_k.shape, bf16),
            jax.ShapeDtypeStruct(leaf_v.shape, bf16),
        ),
        in_specs=[vmem] * 5 + [anywhere] * 3 + [vmem] * 2 + [smem, vmem] + [smem] * 3,
        out_specs=(vmem, vmem, vmem),
        scratch_shapes=[
            pltpu.VMEM((2, N) + shared_k.shape, bf16),
            pltpu.VMEM((heads, N, rows, group * HEAD_SIZE), bf16),
            pltpu.VMEM(weight.shape, bf16),
            pltpu.VMEM((heads, group * rows, HEAD_SIZE), bf16),
            pltpu.VMEM((share, columns, 4 * rows), f32),
            pltpu.VMEM((per_level, columns, 4 * rows), f32),
            pltpu.VMEM((pieces, columns, 4 * rows), bf16),
            pltpu.VMEM((M, share, columns, 4 * rows), bf16),
        ]
        + semaphores(2)
        + semaphores(heads)
        + [dma((pieces,)), dma((M, share)), dma((3,))],
        compiler_params=pltpu.CompilerParams(
            collective_id=0, has_side_effects=True, vmem_limit_bytes=56 * 1024 * 1024
        ),
    )(
        queries, fresh_k, fresh_v, leaf_k, leaf_v, shared_k, shared_v, weight, residual,
        freq, request, positions.reshape(1, rows), parents, lengths, owners,
    )
    results = (hidden, leaf_k_out, leaf_v_out)
    hidden, leaf_k_out, leaf_v_out = pl.pallas_call(
        hand_over,
        out_shape=[jax.ShapeDtypeStruct(r.shape, r.dtype) for r in results],
        in_specs=[vmem] * 3,
        out_specs=[vmem] * 3,
    )(*results)
    return hidden.T, leaf_k_out, leaf_v_out


def solution(mesh):
    both = P("tok", "mlp")
    return jax.shard_map(
        functools.partial(body, mesh.shape["tok"], mesh.shape["mlp"]),
        mesh=mesh,
        in_specs=(both,) * 7 + (P("mlp", "tok"),) * 2 + (P(), P("tok"), P(), P(), P()),
        out_specs=(P("mlp", "tok"), both, both),
        check_vma=False,
    )
```
